128 devices in a mesh: region: 8 (over x, core), cols: 16 (over y, z).
Axes of the slice: x: 4, y: 4, z: 4, core: 2. Of those that a mesh axis runs over, the one named last changes fastest.
Arguments:
- ensemble: float32 [80, 524288], P('cols', 'region'), may hold values from -6 to 6
- obs_value: float32 [64], replicated, may hold values from -6 to 6
- obs_error: float32 [64], replicated, may hold values from 0.25 to 2
- observation_holder: int32 [64], replicated, may hold values from 0 to 127
- obs_column: int32 [64], replicated, may hold values from 0 to 4095
- loc_mask: int32 [64, 8], replicated, may hold values 0 or 1
- loc_taper: float32 [64, 8], replicated, may hold values from 0.2 to 1
Outputs:
- analysis: float32 [80, 524288], P('cols', 'region')
The draws below stay inside these ranges and needn't reach their ends.
All inputs are finite; a program needn't handle non-finite values.
Results may differ from the reference program's by a relative error of at most 0.0003.
Values sent between devices are 32-bit elements; how exact they have to be, the bound alone decides.
No kernel may reach another device: no remote copies, remote signals or barrier semaphores. Data moves between devices by JAX's collectives and lax.ppermute only.
A program may use at most 128 MiB of HBM per device.

```python
import math
import jax
import jax.numpy as jnp
import numpy as np
from jax import lax

MEMBERS = 80
S_DEV = 4096
NOBS = 64
REGION_COLUMNS = 65536
NCOL = 524288
N_REGION = 8
N_COLS = 16


def plant(values, own_key, least, largest):
    longest = values.shape.index(max(values.shape))
    spots = []
    for shift in (0, 1):
        where = [jax.random.randint(jax.random.fold_in(own_key, axis), (), 0, length) for axis, length in enumerate(values.shape)]
        where[longest] = (where[longest] + shift) % values.shape[longest]
        spots.append(tuple(where))
    return values.at[spots[0]].set(least).at[spots[1]].set(largest)


def level_of(stream_key, extent, split, low, top_value):
    def one(position, blocks):
        heights = jax.random.uniform(jax.random.fold_in(jax.random.fold_in(stream_key, 6), position), (blocks,), jnp.float32, low / len(split), top_value / len(split))
        return jnp.repeat(jnp.exp(heights), extent[position] // blocks).reshape((-1,) + (1,) * (len(extent) - position - 1))

    gain = one(*split[0])
    for cut in split[1:]:
        gain = gain * one(*cut)
    return gain


def cumulative_ranks(number_of, slope):
    loads = [(1 << 20) // math.isqrt(standing ** slope) + 1 for standing in range(1, number_of + 1)]
    scale = 1 + sum(loads) // (1 << 30)
    return np.cumsum(np.array([max(1, weight // scale) for weight in loads]))


def ranked(own_key, extent, amount, slope):
    table = cumulative_ranks(amount, slope)
    ticket = jax.random.randint(jax.random.fold_in(own_key, 1), extent, 0, int(table[amount - 1]))
    grade = jnp.searchsorted(jnp.asarray(table, jnp.int32), ticket, side="right")
    return jax.random.permutation(jax.random.fold_in(own_key, 2), amount)[grade].astype(jnp.int32)


def scatter_about(stream_key, shape, width, reach, shards=(), kind=jnp.bfloat16):
    entries = width * jax.random.normal(stream_key, shape, jnp.float32)
    if shards:
        entries = entries * level_of(stream_key, shape, shards, -0.22, 0.18)
    return jnp.clip(entries, -reach, reach).astype(kind)


def setup_inputs(seed: int = 0) -> dict:
    splits = jax.random.split(jax.random.key(seed), 8)
    ensemble = scatter_about(splits[0], (MEMBERS, NCOL), 1.0, 6.0, ((0, 16), (1, 8)), jnp.float32)
    obs_value = scatter_about(splits[1], (NOBS,), 1.5, 6.0, (), jnp.float32)
    obs_error = jnp.clip(jnp.exp(jax.random.uniform(splits[2], (NOBS,), jnp.float32, math.log(0.25), math.log(2.0))), 0.25, 2.0)
    observation_holder = plant(ranked(splits[3], (NOBS,), N_REGION * N_COLS, 2), jax.random.fold_in(splits[3], 3), 0, (N_REGION * N_COLS) - 1).astype(jnp.int32)
    obs_column = plant(jax.random.randint(splits[4], (NOBS,), 0, S_DEV), jax.random.fold_in(splits[4], 1), 0, S_DEV - 1).astype(jnp.int32)
    loc_mask = plant((jax.random.randint(splits[5], (NOBS, N_REGION), 0, 4) < 3).astype(jnp.int32), jax.random.fold_in(splits[5], 1), 0, 1)
    loc_taper = jnp.clip(jax.random.uniform(splits[6], (NOBS, N_REGION), jnp.float32, 0.2, 1.0), 0.2, 1.0)
    return dict(ensemble=ensemble, obs_value=obs_value, obs_error=obs_error, observation_holder=observation_holder, obs_column=obs_column, loc_mask=loc_mask, loc_taper=loc_taper)


highest = lax.Precision.HIGHEST

def assimilate(block, update_transforms, index, value, error, mutual_row, weight_row):
    member_list = block.shape[0]
    prior = lax.dynamic_index_in_dim(block, index, 1, keepdims=False)
    center = jnp.mean(prior)
    spread = prior - center
    variance = jnp.sum(spread * spread) / (member_list - 1)
    summed = variance + error
    scaling = 1.0 / ((member_list - 1) * summed)
    reduction = 1.0 / (1.0 + jnp.sqrt(error / summed))
    shift = value - center - reduction * spread
    later = (jnp.arange(block.shape[1], dtype=jnp.int32) > index).astype(jnp.float32)
    factor = jnp.dot(spread, block, precision=highest) * mutual_row * later * scaling
    block = block + shift[:, None] * factor[None, :]
    project = jnp.einsum('m,rmn->rn', spread, update_transforms, precision=highest)
    update_transforms = update_transforms + (weight_row * scaling)[:, None, None] * shift[None, :, None] * project[:, None, :]
    return (block, update_transforms)

def reference(ensemble, obs_value, obs_error, observation_holder, obs_column, loc_mask, loc_taper):
    member_list = ensemble.shape[0]
    weight = loc_mask.astype(jnp.float32) * loc_taper
    home = observation_holder // N_COLS
    onehot = (home[:, None] == jnp.arange(N_REGION, dtype=jnp.int32)[None, :]).astype(jnp.float32)
    mutual = jnp.dot(weight, onehot.T, precision=highest)
    flat = (observation_holder * S_DEV + obs_column).astype(jnp.int32)
    priors = jnp.take(ensemble, flat, axis=1)
    identity = jnp.broadcast_to(jnp.eye(member_list, dtype=jnp.float32), (N_REGION, member_list, member_list))

    def turn(carry, index):
        block, update_transforms = carry
        block, update_transforms = assimilate(block, update_transforms, index, obs_value[index], obs_error[index], mutual[index], weight[index])
        return ((block, update_transforms), None)
    (priors, update_transforms), _ = lax.scan(turn, (priors, identity), jnp.arange(NOBS, dtype=jnp.int32))
    region_local = ensemble.reshape(member_list, N_REGION, REGION_COLUMNS)
    updated = jnp.einsum('rmn,nrs->mrs', update_transforms, region_local, precision=highest)
    return updated.reshape(member_list, NCOL)
```

```python
import jax
import jax.numpy as jnp
from jax import lax
from jax.experimental import pallas as pl
from jax.experimental.pallas import tpu as pltpu
from jax.sharding import PartitionSpec as P

MEMBERS = 80
NOBS = 64
COLS = 16
REGIONS = 8
OWN = 5
S_DEV = 4096
REGION_COLUMNS = COLS * S_DEV
PIECE = 512
HEAD = OWN * PIECE
TAILS = 3
PADDED = COLS * 8
GROUP = 4
BLOCK = 4

highest = lax.Precision.HIGHEST
SMEM = pl.BlockSpec(memory_space=pltpu.SMEM)
VMEM = pl.BlockSpec(memory_space=pltpu.VMEM)


def params(**more):
    return pltpu.CompilerParams(vmem_limit_bytes=40 << 20, **more)


def split_kernel(where_ref, mine_ref, block_ref, whole_ref, packed_ref, sent_ref, tiles, sems):
    step = pl.program_id(0)

    def fetch(k):
        start = pl.multiple_of((where_ref[k] // 128) * 128, 128)
        return pltpu.make_async_copy(whole_ref.at[:, pl.ds(start, 128)], tiles.at[k], sems.at[k])

    @pl.when(step == 0)
    def _():
        for k in range(NOBS):
            fetch(k).start()

    for b in range(GROUP):
        low = b * S_DEV
        packed_ref[b, 0:OWN, :] = block_ref[:, low : low + HEAD]
        for i in range(TAILS):
            for q in range(OWN):
                at = low + HEAD + i * PIECE
                packed_ref[b, OWN + i : OWN + i + 1, q * PIECE : (q + 1) * PIECE] = block_ref[
                    q : q + 1, at : at + PIECE
                ]

    @pl.when(step == pl.num_programs(0) - 1)
    def _():
        lane = lax.broadcasted_iota(jnp.int32, (OWN, 128), 1)
        got = jnp.zeros((OWN, 128), jnp.float32)
        for k in range(NOBS):
            fetch(k).wait()
            turned = pltpu.roll(tiles[k], lax.rem(k + 128 - lax.rem(where_ref[k], 128), 128), 1)
            got = jnp.where(lane == jnp.where(mine_ref[k] == 1, k, -1), turned, got)
        full = jnp.concatenate([got, jnp.zeros((8 - OWN, 128), jnp.float32)], axis=0)
        sent_ref[...] = jnp.broadcast_to(full[None], sent_ref.shape)


def split(where, mine, ensemble):
    return pl.pallas_call(
        split_kernel,
        grid=(COLS // GROUP,),
        in_specs=[
            SMEM,
            SMEM,
            pl.BlockSpec((OWN, GROUP * S_DEV), lambda s: (0, s)),
            pl.BlockSpec(memory_space=pl.ANY),
        ],
        out_specs=[
            pl.BlockSpec((GROUP, 8, HEAD), lambda s: (s, 0, 0)),
            pl.BlockSpec((REGIONS * COLS, 8, 128), lambda s: (0, 0, 0)),
        ],
        out_shape=[
            jax.ShapeDtypeStruct((COLS, 8, HEAD), jnp.float32),
            jax.ShapeDtypeStruct((REGIONS * COLS, 8, 128), jnp.float32),
        ],
        scratch_shapes=[
            pltpu.VMEM((NOBS, OWN, 128), jnp.float32),
            pltpu.SemaphoreType.DMA((NOBS,)),
        ],
        compiler_params=params(),
        name="split",
    )(where, mine, ensemble, ensemble)


def total(x):
    return jnp.sum(x, axis=0, keepdims=True)


def chain_kernel(value_ref, error_ref, own_ref, got_ref, weight_ref, out_ref, scratch):
    gathered = got_ref[0:COLS]
    for r in range(1, REGIONS):
        gathered = gathered + got_ref[r * COLS : (r + 1) * COLS]
    for c in range(COLS):
        scratch[OWN * c : OWN * (c + 1), :] = gathered[c, 0:OWN, :]
    priors = scratch[...]
    mean = total(priors) * (1.0 / MEMBERS)
    spread = priors - mean
    row = lax.broadcasted_iota(jnp.int32, (MEMBERS, 128), 0)
    lane = lax.broadcasted_iota(jnp.int32, (MEMBERS, 128), 1)
    turn = ((row // OWN) * 8 + lax.rem(row, OWN) == lane).astype(jnp.float32)
    lift = jnp.zeros((1, 128), jnp.float32)
    for low in range(0, NOBS, BLOCK):
        near = range(low, low + BLOCK)
        ps = {k: jnp.broadcast_to(spread[:, k : k + 1], (MEMBERS, 128)) for k in near}
        ms = {k: jnp.broadcast_to(mean[:, k : k + 1], (1, 128)) for k in near}
        for j in near:
            p = ps[j]
            e = error_ref[j]
            s = total(p * p) * (1.0 / (MEMBERS - 1)) + e
            scaling = 1.0 / ((MEMBERS - 1) * s)
            damped = 1.0 / ((MEMBERS - 1) * (s + jnp.sqrt(e * s)))
            move = (value_ref[j] - ms[j]) * scaling
            for k in range(j + 1, low + BLOCK):
                w = jnp.broadcast_to(weight_ref[j : j + 1, k : k + 1], (1, 128))
                f = w * total(p * ps[k])
                ps[k] = ps[k] - p * (f * damped)
                ms[k] = ms[k] + move * f
            f = weight_ref[j : j + 1, :] * total(p * spread)
            h = own_ref[j] * total(p * turn)
            spread = spread - p * (f * damped)
            turn = turn - p * (h * damped)
            mean = mean + move * f
            lift = lift + move * h
    turn = turn + lift
    for c in range(COLS):
        out_ref[8 * c : 8 * c + OWN, :] = turn[OWN * c : OWN * (c + 1), :]
        out_ref[8 * c + OWN : 8 * (c + 1), :] = jnp.zeros((8 - OWN, 128), jnp.float32)


def chain(value, error, own, got, weight):
    return pl.pallas_call(
        chain_kernel,
        in_specs=[SMEM, SMEM, SMEM, VMEM, VMEM],
        out_specs=VMEM,
        out_shape=jax.ShapeDtypeStruct((PADDED, 128), jnp.float32),
        scratch_shapes=[pltpu.VMEM((MEMBERS, 128), jnp.float32)],
        compiler_params=params(),
        cost_estimate=pl.CostEstimate(flops=20_000_000, bytes_accessed=20_000_000, transcendentals=0),
        name="chain",
    )(value, error, own, got, weight)


def apply_kernel(turn_ref, got_ref, out_ref, tail):
    turn = turn_ref[...]
    for q in range(OWN):
        span = slice(q * PIECE, (q + 1) * PIECE)
        x = got_ref[:, :, span].reshape(PADDED, PIECE)
        y = jnp.dot(turn, x, precision=highest, preferred_element_type=jnp.float32)
        out_ref[:, 0:OWN, span] = y.reshape(COLS, 8, PIECE)[:, 0:OWN]
    for i in range(TAILS):
        tail[...] = jnp.zeros_like(tail)
        for q in range(OWN):
            for c in range(COLS):
                tail[8 * c + q : 8 * c + q + 1, :] = got_ref[
                    c, OWN + i : OWN + i + 1, q * PIECE : (q + 1) * PIECE
                ]
        y = jnp.dot(turn, tail[...], precision=highest, preferred_element_type=jnp.float32)
        for q in range(OWN):
            for c in range(COLS):
                out_ref[c, OWN + i : OWN + i + 1, q * PIECE : (q + 1) * PIECE] = y[
                    8 * c + q : 8 * c + q + 1, :
                ]


def apply(turn, got):
    return pl.pallas_call(
        apply_kernel,
        in_specs=[VMEM, VMEM],
        out_specs=VMEM,
        out_shape=jax.ShapeDtypeStruct((COLS, 8, HEAD), jnp.float32),
        scratch_shapes=[pltpu.VMEM((PADDED, PIECE), jnp.float32)],
        compiler_params=params(),
        name="apply",
    )(turn, got)


def join_kernel(packed_ref, out_ref):
    for b in range(GROUP):
        low = b * S_DEV
        out_ref[:, low : low + HEAD] = packed_ref[b, 0:OWN, :]
        for i in range(TAILS):
            for q in range(OWN):
                at = low + HEAD + i * PIECE
                out_ref[q : q + 1, at : at + PIECE] = packed_ref[
                    b, OWN + i : OWN + i + 1, q * PIECE : (q + 1) * PIECE
                ]


def join(packed):
    return pl.pallas_call(
        join_kernel,
        grid=(COLS // GROUP,),
        in_specs=[pl.BlockSpec((GROUP, 8, HEAD), lambda s: (s, 0, 0))],
        out_specs=pl.BlockSpec((OWN, GROUP * S_DEV), lambda s: (0, s)),
        out_shape=jax.ShapeDtypeStruct((OWN, REGION_COLUMNS), jnp.float32),
        compiler_params=params(),
        name="join",
    )(packed)


def per_device(ensemble, obs_value, obs_error, observation_holder, obs_column, loc_mask, loc_taper):
    region = lax.axis_index("region")
    weight = loc_mask.astype(jnp.float32) * loc_taper
    home = observation_holder // COLS
    mine = (home == region).astype(jnp.int32)
    where = (observation_holder - home * COLS) * S_DEV + obs_column
    mutual = jnp.zeros((NOBS, NOBS), jnp.float32)
    for r in range(REGIONS):
        mutual = jnp.where(home[None, :] == r, weight[:, r : r + 1], mutual)
    mutual = jnp.pad(mutual, ((0, 0), (0, 128 - NOBS)))
    own = lax.dynamic_index_in_dim(weight, region, 1, keepdims=False)
    packed, sent = split(where, mine, ensemble)
    state = lax.all_to_all(packed, "cols", 0, 0)
    got = lax.all_to_all(sent, ("region", "cols"), 0, 0)
    turn = chain(obs_value, obs_error, own, got, mutual)
    state = apply(turn, state)
    state = lax.all_to_all(state, "cols", 0, 0)
    return join(state)


def solution(mesh):
    placed = (P("cols", "region"), P(), P(), P(), P(), P(), P())
    return jax.shard_map(
        per_device, mesh=mesh, in_specs=placed, out_specs=P("cols", "region"), check_vma=False
    )
```

```python
import jax
import jax.numpy as jnp
from jax import lax
from jax.experimental import pallas as pl
from jax.experimental.pallas import tpu as pltpu
from jax.sharding import PartitionSpec as P

MEMBERS = 80
NOBS = 64
COLS = 16
REGIONS = 8
OWN = 5
S_DEV = 4096
REGION_COLUMNS = COLS * S_DEV
PIECE = 512
HEAD = OWN * PIECE
TAILS = 3
PADDED = COLS * 8
GROUP = 4
BLOCK = 4

highest = lax.Precision.HIGHEST
SMEM = pl.BlockSpec(memory_space=pltpu.SMEM)
VMEM = pl.BlockSpec(memory_space=pltpu.VMEM)


def params(**more):
    return pltpu.CompilerParams(vmem_limit_bytes=40 << 20, **more)


def gather_kernel(holder_ref, column_ref, whole_ref, out_ref, tiles, sems):
    region = lax.axis_index("region")

    def fetch(k):
        start = lax.bitwise_and(holder_ref[k], COLS - 1) * S_DEV + lax.bitwise_and(column_ref[k], -128)
        start = pl.multiple_of(start, 128)
        return pltpu.make_async_copy(whole_ref.at[:, pl.ds(start, 128)], tiles.at[k], sems.at[k])

    for k in range(NOBS):
        fetch(k).start()
    for k in range(NOBS):
        fetch(k).wait()
    lane = lax.broadcasted_iota(jnp.int32, (OWN, 128), 1)
    got = jnp.zeros((OWN, 128), jnp.float32)
    for k in range(NOBS):
        turned = pltpu.roll(tiles[k], lax.bitwise_and(k - column_ref[k], 127), 1)
        home = lax.shift_right_logical(holder_ref[k], 4)
        got = jnp.where(lane == jnp.where(home == region, k, -1), turned, got)
    full = jnp.concatenate([got, jnp.zeros((8 - OWN, 128), jnp.float32)], axis=0)
    out_ref[...] = jnp.broadcast_to(full[None], out_ref.shape)


def gather(holder, column, ensemble):
    return pl.pallas_call(
        gather_kernel,
        in_specs=[SMEM, SMEM, pl.BlockSpec(memory_space=pltpu.HBM)],
        out_specs=VMEM,
        out_shape=jax.ShapeDtypeStruct((REGIONS, 8, 128), jnp.float32),
        scratch_shapes=[
            pltpu.VMEM((NOBS, OWN, 128), jnp.float32),
            pltpu.SemaphoreType.DMA((NOBS,)),
        ],
        compiler_params=params(),
        name="gather",
    )(holder, column, ensemble)


def pack_kernel(block_ref, packed_ref):
    for b in range(GROUP):
        low = b * S_DEV
        packed_ref[b, 0:OWN, :] = block_ref[:, low : low + HEAD]
        for i in range(TAILS):
            for q in range(OWN):
                at = low + HEAD + i * PIECE
                packed_ref[b, OWN + i : OWN + i + 1, q * PIECE : (q + 1) * PIECE] = block_ref[
                    q : q + 1, at : at + PIECE
                ]


def pack(ensemble):
    return pl.pallas_call(
        pack_kernel,
        grid=(COLS // GROUP,),
        in_specs=[pl.BlockSpec((OWN, GROUP * S_DEV), lambda s: (0, s))],
        out_specs=pl.BlockSpec((GROUP, 8, HEAD), lambda s: (s, 0, 0)),
        out_shape=jax.ShapeDtypeStruct((COLS, 8, HEAD + 128), jnp.float32),
        compiler_params=params(),
        name="pack",
    )(ensemble)


def place_kernel(got_ref, packed_ref, out_ref, copies, sem):
    copies[...] = jnp.broadcast_to(jnp.sum(got_ref[...], axis=0)[None], copies.shape)
    move = pltpu.make_async_copy(copies, out_ref.at[:, :, pl.ds(HEAD, 128)], sem)
    move.start()
    move.wait()


def place(got, packed):
    return pl.pallas_call(
        place_kernel,
        in_specs=[VMEM, pl.BlockSpec(memory_space=pl.ANY)],
        out_specs=pl.BlockSpec(memory_space=pl.ANY),
        out_shape=jax.ShapeDtypeStruct(packed.shape, jnp.float32),
        input_output_aliases={1: 0},
        scratch_shapes=[pltpu.VMEM((COLS, 8, 128), jnp.float32), pltpu.SemaphoreType.DMA],
        compiler_params=params(),
        name="place",
    )(got, packed)


def total(x):
    return jnp.sum(x, axis=0, keepdims=True)


def chain_kernel(value_ref, error_ref, own_ref, got_ref, weight_ref, out_ref, scratch):
    for c in range(COLS):
        scratch[OWN * c : OWN * (c + 1), :] = got_ref[c, 0:OWN, :]
    priors = scratch[...]
    mean = total(priors) * (1.0 / MEMBERS)
    spread = priors - mean
    row = lax.broadcasted_iota(jnp.int32, (MEMBERS, 128), 0)
    lane = lax.broadcasted_iota(jnp.int32, (MEMBERS, 128), 1)
    turn = ((row // OWN) * 8 + lax.rem(row, OWN) == lane).astype(jnp.float32)
    lift = jnp.zeros((1, 128), jnp.float32)
    for low in range(0, NOBS, BLOCK):
        near = range(low, low + BLOCK)
        ps = {k: jnp.broadcast_to(spread[:, k : k + 1], (MEMBERS, 128)) for k in near}
        ms = {k: jnp.broadcast_to(mean[:, k : k + 1], (1, 128)) for k in near}
        for j in near:
            p = ps[j]
            e = error_ref[j]
            s = total(p * p) * (1.0 / (MEMBERS - 1)) + e
            scaling = 1.0 / ((MEMBERS - 1) * s)
            damped = 1.0 / ((MEMBERS - 1) * (s + jnp.sqrt(e * s)))
            move = (value_ref[j] - ms[j]) * scaling
            for k in range(j + 1, low + BLOCK):
                w = jnp.broadcast_to(weight_ref[j : j + 1, k : k + 1], (1, 128))
                f = w * total(p * ps[k])
                ps[k] = ps[k] - p * (f * damped)
                ms[k] = ms[k] + move * f
            f = weight_ref[j : j + 1, :] * total(p * spread)
            h = own_ref[j] * total(p * turn)
            spread = spread - p * (f * damped)
            turn = turn - p * (h * damped)
            mean = mean + move * f
            lift = lift + move * h
    turn = turn + lift
    for c in range(COLS):
        out_ref[8 * c : 8 * c + OWN, :] = turn[OWN * c : OWN * (c + 1), :]
        out_ref[8 * c + OWN : 8 * (c + 1), :] = jnp.zeros((8 - OWN, 128), jnp.float32)


def chain(value, error, own, got, weight):
    return pl.pallas_call(
        chain_kernel,
        grid=(1,),
        in_specs=[SMEM, SMEM, SMEM, pl.BlockSpec((COLS, 8, 128), lambda s: (0, 0, HEAD // 128)), VMEM],
        out_specs=VMEM,
        out_shape=jax.ShapeDtypeStruct((PADDED, 128), jnp.float32),
        scratch_shapes=[pltpu.VMEM((MEMBERS, 128), jnp.float32)],
        compiler_params=params(),
        name="chain",
    )(value, error, own, got, weight)


def apply_kernel(turn_ref, got_ref, out_ref, tail):
    turn = turn_ref[...]
    for q in range(OWN):
        span = slice(q * PIECE, (q + 1) * PIECE)
        x = got_ref[:, :, span].reshape(PADDED, PIECE)
        y = jnp.dot(turn, x, precision=highest, preferred_element_type=jnp.float32)
        out_ref[:, 0:OWN, span] = y.reshape(COLS, 8, PIECE)[:, 0:OWN]
    for i in range(TAILS):
        tail[...] = jnp.zeros_like(tail)
        for q in range(OWN):
            for c in range(COLS):
                tail[8 * c + q : 8 * c + q + 1, :] = got_ref[
                    c, OWN + i : OWN + i + 1, q * PIECE : (q + 1) * PIECE
                ]
        y = jnp.dot(turn, tail[...], precision=highest, preferred_element_type=jnp.float32)
        for q in range(OWN):
            for c in range(COLS):
                out_ref[c, OWN + i : OWN + i + 1, q * PIECE : (q + 1) * PIECE] = y[
                    8 * c + q : 8 * c + q + 1, :
                ]


def apply(turn, got):
    return pl.pallas_call(
        apply_kernel,
        in_specs=[VMEM, VMEM],
        out_specs=VMEM,
        out_shape=jax.ShapeDtypeStruct((COLS, 8, HEAD), jnp.float32),
        scratch_shapes=[pltpu.VMEM((PADDED, PIECE), jnp.float32)],
        compiler_params=params(),
        name="apply",
    )(turn, got)


def join_kernel(packed_ref, out_ref):
    for b in range(GROUP):
        low = b * S_DEV
        out_ref[:, low : low + HEAD] = packed_ref[b, 0:OWN, :]
        for i in range(TAILS):
            for q in range(OWN):
                at = low + HEAD + i * PIECE
                out_ref[q : q + 1, at : at + PIECE] = packed_ref[
                    b, OWN + i : OWN + i + 1, q * PIECE : (q + 1) * PIECE
                ]


def join(packed):
    return pl.pallas_call(
        join_kernel,
        grid=(COLS // GROUP,),
        in_specs=[pl.BlockSpec((GROUP, 8, HEAD), lambda s: (s, 0, 0))],
        out_specs=pl.BlockSpec((OWN, GROUP * S_DEV), lambda s: (0, s)),
        out_shape=jax.ShapeDtypeStruct((OWN, REGION_COLUMNS), jnp.float32),
        compiler_params=params(),
        name="join",
    )(packed)


def per_device(ensemble, obs_value, obs_error, observation_holder, obs_column, loc_mask, loc_taper):
    region = lax.axis_index("region")
    weight = loc_mask.astype(jnp.float32) * loc_taper
    home = observation_holder // COLS
    mutual = jnp.zeros((NOBS, NOBS), jnp.float32)
    for r in range(REGIONS):
        mutual = jnp.where(home[None, :] == r, weight[:, r : r + 1], mutual)
    mutual = jnp.pad(mutual, ((0, 0), (0, 128 - NOBS)))
    own = lax.dynamic_index_in_dim(weight, region, 1, keepdims=False)
    priors = gather(observation_holder, obs_column, ensemble)
    packed = pack(ensemble)
    priors = lax.all_to_all(priors, "region", 0, 0)
    state = lax.all_to_all(place(priors, packed), "cols", 0, 0)
    turn = chain(obs_value, obs_error, own, state, mutual)
    state = apply(turn, state)
    state = lax.all_to_all(state, "cols", 0, 0)
    return join(state)


def solution(mesh):
    placed = (P("cols", "region"), P(), P(), P(), P(), P(), P())
    return jax.shard_map(
        per_device, mesh=mesh, in_specs=placed, out_specs=P("cols", "region"), check_vma=False
    )
```

```python
import jax
import jax.numpy as jnp
from jax import lax
from jax.experimental import pallas as pl
from jax.experimental.pallas import tpu as pltpu
from jax.sharding import PartitionSpec as P

MEMBERS = 80
NOBS = 64
COLS = 16
REGIONS = 8
OWN = 5
S_DEV = 4096
REGION_COLUMNS = COLS * S_DEV
HALF = S_DEV // 2
PIECE = S_DEV // 8
FULL = HALF + PIECE
PADDED = COLS * 8
BLOCK = 4
SPARE = MEMBERS - 1

SMEM = pl.BlockSpec(memory_space=pltpu.SMEM)
VMEM = pl.BlockSpec(memory_space=pltpu.VMEM)
HBM = pl.BlockSpec(memory_space=pltpu.HBM)


def params(size=40 << 20):
    return pltpu.CompilerParams(vmem_limit_bytes=size)


def split_kernel(
    holder_ref, column_ref, whole_ref, row_ref, mask_ref, taper_ref, packed_ref, out_ref, weight_ref,
    held, holders, columns, row, mask, taper, sems, small_sems
):
    region = lax.axis_index("region")
    small = [(holder_ref, holders), (column_ref, columns), (row_ref, row), (mask_ref, mask), (taper_ref, taper)]
    small = [pltpu.make_async_copy(a, b, small_sems.at[n]) for n, (a, b) in enumerate(small)]

    def fetch(b):
        part = pl.ds(b * S_DEV, S_DEV)
        return pltpu.make_async_copy(whole_ref.at[:, part], held.at[:, part], sems.at[b])

    for copy in small:
        copy.start()
    for b in range(COLS):
        fetch(b).start()
    for copy in small:
        copy.wait()
    weight = (mask[...].astype(jnp.float32) * taper[...]).T
    home = lax.shift_right_logical(row[...], 4)
    mutual = jnp.zeros((NOBS, NOBS), jnp.float32)
    own = jnp.zeros((NOBS, 128), jnp.float32)
    for r in range(REGIONS):
        column = weight[:, r : r + 1]
        mutual = jnp.where(home == r, jnp.broadcast_to(column, (NOBS, NOBS)), mutual)
        own = jnp.where(region == r, jnp.broadcast_to(column, (NOBS, 128)), own)
    weight_ref[0] = jnp.concatenate([mutual, jnp.zeros((NOBS, 128 - NOBS), jnp.float32)], axis=1)
    weight_ref[1] = own
    for b in range(COLS):
        fetch(b).wait()
        low = b * S_DEV
        first = held[0:4, low : low + HALF]
        second = held[0:4, low + HALF : low + S_DEV]
        packed_ref[b, :, 0:HALF] = jnp.concatenate([first, second], axis=0)
        last = [held[4:5, low + s * PIECE : low + (s + 1) * PIECE] for s in range(8)]
        packed_ref[b, :, HALF:FULL] = jnp.concatenate(last, axis=0)
    lane = lax.broadcasted_iota(jnp.int32, (OWN, 128), 1)
    got = jnp.zeros((OWN, 128), jnp.float32)
    for k in range(NOBS):
        holder, column = holders[k], columns[k]
        start = lax.bitwise_and(holder, COLS - 1) * S_DEV + lax.bitwise_and(column, S_DEV - 128)
        tile = held[:, pl.ds(pl.multiple_of(start, 128), 128)]
        turned = pltpu.roll(tile, lax.bitwise_and(k - column, 127), 1)
        at = jnp.where(lax.shift_right_logical(holder, 4) == region, k, -1)
        got = jnp.where(lane == at, turned, got)
    full = jnp.concatenate([got, jnp.zeros((8 - OWN, 128), jnp.float32)], axis=0)
    out_ref[...] = jnp.broadcast_to(full[None], out_ref.shape)


def split(*inputs):
    return pl.pallas_call(
        split_kernel,
        in_specs=[HBM] * 6,
        out_specs=[VMEM] * 3,
        out_shape=[
            pltpu.VMEM((COLS, 8, FULL + 128), jnp.float32),
            pltpu.VMEM((REGIONS, 8, 128), jnp.float32),
            pltpu.VMEM((2, NOBS, 128), jnp.float32),
        ],
        scratch_shapes=[
            pltpu.VMEM((OWN, REGION_COLUMNS), jnp.float32),
            pltpu.SMEM((NOBS,), jnp.int32),
            pltpu.SMEM((NOBS,), jnp.int32),
            pltpu.VMEM((1, NOBS), jnp.int32),
            pltpu.VMEM((REGIONS, NOBS), jnp.int32),
            pltpu.VMEM((REGIONS, NOBS), jnp.float32),
            pltpu.SemaphoreType.DMA((COLS,)),
            pltpu.SemaphoreType.DMA((5,)),
        ],
        compiler_params=params(),
        name="split",
    )(*[pltpu.with_memory_space_constraint(x, pltpu.HBM) for x in inputs])


def place_kernel(got_ref, packed_ref, out_ref, copies, sem):
    copies[...] = jnp.broadcast_to(jnp.sum(got_ref[...], axis=0)[None], copies.shape)
    move = pltpu.make_async_copy(copies, out_ref.at[:, :, pl.ds(FULL, 128)], sem)
    move.start()
    move.wait()


def place(got, packed):
    return pl.pallas_call(
        place_kernel,
        in_specs=[VMEM, pl.BlockSpec(memory_space=pl.ANY)],
        out_specs=pl.BlockSpec(memory_space=pl.ANY),
        out_shape=jax.ShapeDtypeStruct(packed.shape, jnp.float32),
        input_output_aliases={1: 0},
        scratch_shapes=[pltpu.VMEM((COLS, 8, 128), jnp.float32), pltpu.SemaphoreType.DMA],
        compiler_params=params(),
        name="place",
    )(got, packed)


def total(x):
    return jnp.sum(x, axis=0, keepdims=True)


def spread_out(x, shape):
    return jnp.broadcast_to(x, shape)


def chain(value_ref, error_ref, got_ref, weight_ref, scratch, aside):
    for c in range(COLS):
        scratch[OWN * c : OWN * (c + 1), :] = got_ref[c, 0:OWN, FULL : FULL + 128]
    priors = scratch[...]
    mean = total(priors) * (1.0 / MEMBERS)
    spread = priors - mean
    row = lax.broadcasted_iota(jnp.int32, (MEMBERS, 128), 0)
    lane = lax.broadcasted_iota(jnp.int32, (MEMBERS, 128), 1)
    turn = ((row // OWN) * 8 + lax.rem(row, OWN) == lane).astype(jnp.float32)
    lift = jnp.zeros((1, 128), jnp.float32)
    for low in range(0, NOBS, BLOCK):
        near = range(BLOCK)
        p, m, w, dots, d0, d1, c0, c1 = {}, {}, {}, {}, {}, {}, {}, {}
        for j in near:
            p[j] = jnp.broadcast_to(spread[:, low + j : low + j + 1], (MEMBERS, 128))
            m[j] = jnp.broadcast_to(mean[:, low + j : low + j + 1], (1, 128))
            for k in range(j + 1, BLOCK):
                at = weight_ref[0, low + j : low + j + 1, low + k : low + k + 1]
                w[j, k] = jnp.broadcast_to(at, (1, 128))
        for j in near:
            for k in range(j, BLOCK):
                dots[j, k] = total(p[j] * p[k])
            d0[j] = total(p[j] * spread)
            d1[j] = total(p[j] * turn)
        aside(low // BLOCK)
        for j in near:
            e = error_ref[low + j]
            own = dots[j, j]
            s = own * (1.0 / SPARE) + e
            root = jnp.sqrt(jnp.full((1, 128), e, jnp.float32))
            damped = 1.0 / (SPARE * (s + root * (s * lax.rsqrt(s))))
            move = (value_ref[low + j] - m[j]) * (1.0 / (SPARE * s))
            f0 = weight_ref[0, low + j : low + j + 1, :] * d0[j]
            f1 = weight_ref[1, low + j : low + j + 1, :] * d1[j]
            c0[j] = f0 * damped
            c1[j] = f1 * damped
            mean = mean + move * f0
            lift = lift + move * f1
            a = {}
            for k in range(j + 1, BLOCK):
                f = w[j, k] * dots[j, k]
                a[k] = f * damped
                m[k] = m[k] + move * f
            for k in range(j + 1, BLOCK):
                t = dots[j, k] - a[k] * own
                for l in range(k, BLOCK):
                    dots[k, l] = dots[k, l] - a[k] * dots[j, l] - a[l] * t
                d0[k] = d0[k] - a[k] * d0[j] - t * c0[j]
                d1[k] = d1[k] - a[k] * d1[j] - t * c1[j]
                p[k] = p[k] - a[k] * p[j]
        for j in near:
            spread = spread - p[j] * c0[j]
            turn = turn - p[j] * c1[j]
    return turn + lift


def halves(x):
    high = x.astype(jnp.bfloat16)
    return high, (x - high.astype(jnp.float32)).astype(jnp.bfloat16)


def turn_lanes(x):
    lane = lax.rem(lax.broadcasted_iota(jnp.int32, x.shape, 1), 8)
    return jnp.where(lane < 4, pltpu.roll(x, x.shape[1] - 4, 1), pltpu.roll(x, 4, 1))


def apply_kernel(value_ref, error_ref, got_ref, weight_ref, out_ref, scratch, wide, parts):
    row = lax.broadcasted_iota(jnp.int32, (8, PIECE), 0)

    def span(s):
        return slice((s % 4) * PIECE, (s % 4 + 1) * PIECE)

    def unpack(s):
        for c in range(COLS):
            last = got_ref[c, :, HALF:FULL]
            to = 4 if s < 4 else 0
            last = pltpu.roll(last, (to - s) % 8, 0) if (to - s) % 8 else last
            x = jnp.where(row == to, last, got_ref[c, :, span(s)])
            parts[s, 8 * c : 8 * (c + 1), :] = x
        high, low = halves(parts[s])
        wide[s, 0:PADDED, :] = high
        wide[s, PADDED : 2 * PADDED, :] = low

    def aside(n):
        if n % 2 == 0:
            unpack(n // 2)

    turn = chain(value_ref, error_ref, got_ref, weight_ref, scratch, aside)
    square = jnp.zeros((PADDED, 128), jnp.float32)
    rows = []
    for c in range(COLS):
        rows += [turn[OWN * c : OWN * (c + 1), :], jnp.zeros((8 - OWN, 128), jnp.float32)]
    square = jnp.concatenate(rows, axis=0)
    turned = turn_lanes(square)
    for n, q in enumerate((square, turned)):
        high, low = halves(q)
        twice = jnp.concatenate([high, high], axis=1)
        for s in range(4 * n, 4 * n + 4):
            y = jnp.dot(twice, wide[s], preferred_element_type=jnp.float32)
            y = y + jnp.dot(low, wide[s, 0:PADDED, :], preferred_element_type=jnp.float32)
            y = y.reshape(COLS, 8, PIECE)
            if n == 0:
                out_ref[:, 0:4, span(s)] = y[:, 0:4]
            else:
                out_ref[:, 4:8, span(s)] = y[:, 0:4]
            out_ref[:, s : s + 1, HALF:FULL] = y[:, 4:5]


def apply(value, error, got, weight):
    return pl.pallas_call(
        apply_kernel,
        in_specs=[SMEM, SMEM, VMEM, VMEM],
        out_specs=VMEM,
        out_shape=jax.ShapeDtypeStruct((COLS, 8, FULL), jnp.float32),
        scratch_shapes=[
            pltpu.VMEM((MEMBERS, 128), jnp.float32),
            pltpu.VMEM((8, 2 * PADDED, PIECE), jnp.bfloat16),
            pltpu.VMEM((8, PADDED, PIECE), jnp.float32),
        ],
        compiler_params=params(),
        name="apply",
    )(value, error, got, weight)


def join_kernel(packed_ref, out_ref, held, sems):
    def send(b):
        part = pl.ds(b * S_DEV, S_DEV)
        return pltpu.make_async_copy(held.at[:, part], out_ref.at[:, part], sems.at[b])

    for b in range(COLS):
        low = b * S_DEV
        for s in range(8):
            at = (s % 4) * PIECE
            first = packed_ref[b, 0:4, at : at + PIECE]
            if s >= 4:
                first = packed_ref[b, 4:8, at : at + PIECE]
            last = packed_ref[b, s : s + 1, HALF:FULL]
            at = low + s * PIECE
            held[:, at : at + PIECE] = jnp.concatenate([first, last], axis=0)
        send(b).start()
    for b in range(COLS):
        send(b).wait()


def join(packed):
    return pl.pallas_call(
        join_kernel,
        in_specs=[VMEM],
        out_specs=pl.BlockSpec(memory_space=pl.ANY),
        out_shape=jax.ShapeDtypeStruct((OWN, REGION_COLUMNS), jnp.float32),
        scratch_shapes=[
            pltpu.VMEM((OWN, REGION_COLUMNS), jnp.float32),
            pltpu.SemaphoreType.DMA((COLS,)),
        ],
        compiler_params=params(),
        name="join",
    )(packed)


def per_device(ensemble, obs_value, obs_error, observation_holder, obs_column, loc_mask, loc_taper):
    row = observation_holder.reshape(1, NOBS)
    packed, priors, weight = split(
        observation_holder, obs_column, ensemble, row, loc_mask.T, loc_taper.T
    )
    priors = lax.all_to_all(priors, "region", 0, 0)
    state = lax.all_to_all(place(priors, packed), "cols", 0, 0)
    state = apply(obs_value, obs_error, state, weight)
    state = lax.all_to_all(state, "cols", 0, 0)
    return join(state)


def solution(mesh):
    placed = (P("cols", "region"), P(), P(), P(), P(), P(), P())
    return jax.shard_map(
        per_device, mesh=mesh, in_specs=placed, out_specs=P("cols", "region"), check_vma=False
    )
```
